32 devices in a mesh: rep: 8 (over y, x, core), fsdp: 4 (over z).
Axes of the slice: x: 2, y: 2, z: 4, core: 2. Of those that a mesh axis runs over, the one named last changes fastest.
Arguments:
- weights: bfloat16 [8, 4096, 2048], P('rep', None, 'fsdp'), may hold values from -6 to 6
- momentum: float32 [8, 4096, 2048], P('rep', None, 'fsdp'), may hold values from -6 to 6
- states: bfloat16 [2, 8, 512, 4096], P(None, 'rep', 'fsdp')
- plan: int32 [2], replicated, may hold values from 1 to 4, as said below
Outputs:
- changes: bfloat16 [2, 8, 4096, 2048], P(None, 'rep', None, 'fsdp')
The draws below stay inside these ranges and needn't reach their ends.
Inputs may be any that keep to these rules, and one draw needn't show every extreme that they name: `plan`: every entry is a power of two, one entry is 4 and the other entries are smaller.
All inputs are finite; a program needn't handle non-finite values.
Results may differ from the reference program's by a relative error of at most 0.008.
Values may be sent and summed in bfloat16 or wider, within the bound.
A program may use at most 128 MiB of HBM per device.

```python
import math
import jax
import jax.numpy as jnp
from jax import lax

D = 4096
OUTW = 2048
STEPS = 2
TOK_REP = 512
REPS = 8


def draw_states(key, part):
    key = jax.random.fold_in(key, 2)
    keys = jax.random.split(key, 3)
    shape_all = (STEPS, REPS, TOK_REP, D)
    column_index = jnp.arange(D, dtype=jnp.float32)
    column_scale = jnp.exp(math.log(3.0) * column_index / OUTW + math.log(2.5) * jax.random.uniform(keys[1], (D,), jnp.float32))
    base = jnp.clip(jax.random.normal(keys[0], shape_all, jnp.float32), -6.0, 6.0)
    row_scale = jnp.exp(math.log(10.0) * jax.random.uniform(keys[2], (STEPS, REPS, TOK_REP, 1), jnp.float32))
    return (base * column_scale * row_scale).astype(jnp.bfloat16)


def draw_plan(key, part):
    key = jax.random.fold_in(key, 1)
    keys = jax.random.split(key, 2)
    levels = REPS.bit_length() - 1
    exponents = jax.random.randint(keys[0], (STEPS,), 0, levels - 1)
    chosen = jax.random.randint(keys[1], (), 0, STEPS)
    exponents = jnp.where(jnp.arange(STEPS) == chosen, levels - 1, exponents)
    return jnp.left_shift(jnp.ones((STEPS,), jnp.int32), exponents.astype(jnp.int32)).astype(jnp.int32)


def steps_of(own_key, shape, shards, low, largest):
    loudness = 1.0
    for axis_at, shards_of in shards:
        heights = jax.random.uniform(jax.random.fold_in(jax.random.fold_in(own_key, 6), axis_at), (shards_of,), jnp.float32, low / len(shards), largest / len(shards))
        loudness = loudness * jnp.repeat(jnp.exp(heights), shape[axis_at] // shards_of).reshape((-1,) + (1,) * (len(shape) - 1 - axis_at))
    return loudness


def normal_values(rng, extent, scale, limit, cuts=(), held_as=jnp.bfloat16):
    values = scale * jax.random.normal(rng, extent, jnp.float32)
    if cuts:
        values = values * steps_of(rng, extent, cuts, -0.22, 0.18)
    return jnp.clip(values, -limit, limit).astype(held_as)


def setup_inputs(seed: int = 0) -> dict:
    key_list = jax.random.split(jax.random.key(seed), 5)
    weights = normal_values(key_list[0], (REPS, D, OUTW), 1.0, 6.0, ((0, 8), (2, 4)))
    momentum = normal_values(key_list[1], (REPS, D, OUTW), 1.0, 6.0, ((0, 8), (2, 4)), jnp.float32)
    states = draw_states(jax.random.fold_in(key_list[4], 71), 0)
    plan = draw_plan(jax.random.fold_in(key_list[4], 71), 0)
    return dict(weights=weights, momentum=momentum, states=states, plan=plan)


def normalize(row_block):
    values = row_block.astype(jnp.float32)
    return (values * lax.rsqrt(lax.optimization_barrier(jnp.mean(values * values, axis=-1, keepdims=True)) + 1e-06)).astype(jnp.bfloat16)

def replica_gradient(weight_one, state_rows):
    scale_in = 1.0 / D ** 0.5
    normed = normalize(state_rows)
    window = state_rows[:, :OUTW].astype(jnp.float32)
    predicted = jnp.dot(normed, weight_one, preferred_element_type=jnp.float32) * scale_in + window
    residual = jnp.concatenate([predicted[:-1] - window[1:], jnp.zeros((1, OUTW), jnp.float32)], 0)
    residual = residual.astype(jnp.bfloat16)
    return jnp.dot(normed.T, residual, preferred_element_type=jnp.float32) * scale_in

def replica_step(operands):
    weight_one, moment_one, weight_other, moment_other, state_rows = operands
    gradient = replica_gradient(weight_one, state_rows)
    square_sum = jnp.sum(gradient * gradient)
    update = gradient * lax.rsqrt(square_sum / (D * OUTW) + 1e-06)
    mean_weight = 0.5 * (weight_one.astype(jnp.float32) + weight_other.astype(jnp.float32))
    mean_moment = 0.5 * (moment_one + moment_other)
    moment_next = 0.9 * mean_moment + update
    weight_next = (mean_weight - 0.1 * moment_next).astype(jnp.bfloat16)
    change = (weight_next.astype(jnp.float32) - weight_one.astype(jnp.float32)).astype(jnp.bfloat16)
    return (weight_next, moment_next, change)

def reference(weights, momentum, states, plan):
    weight_now = weights
    moment_now = momentum
    replica_ids = jnp.arange(REPS, dtype=jnp.int32)
    outputs = []
    for step_index in range(STEPS):
        partner = jnp.bitwise_xor(replica_ids, plan[step_index].astype(jnp.int32))
        weight_now, moment_now, change = lax.map(replica_step, (weight_now, moment_now, weight_now[partner], moment_now[partner], states[step_index]))
        outputs.append(change)
    return jnp.stack(outputs)
```

```python
from functools import partial
import math

import jax
import jax.numpy as jnp
from jax import lax
from jax.sharding import PartitionSpec as P

step_size = 0.1
moment_keep = 0.9
pair_keep = 0.5 * moment_keep
f32 = jnp.float32
bf16 = jnp.bfloat16


def swapped(value, bit):
    mask = 2**bit
    pairs = [(source, source ^ mask) for source in range(lax.axis_size("rep"))]
    return lax.ppermute(value, "rep", pairs)


def normalize(row_block):
    values = row_block.astype(f32)
    return (values * lax.rsqrt(jnp.mean(values * values, axis=-1, keepdims=True) + 1e-06)).astype(bf16)


def fsdp_sum(value):
    size = lax.axis_size("fsdp")
    tile = jnp.full((8, 128), value, f32)
    total = tile
    for shift in range(1, size):
        total = total + lax.ppermute(tile, "fsdp", [(s, (s + shift) % size) for s in range(size)])
    return total[0, 0]


def gradient_of(rows, weight):
    depth, width = weight.shape
    scale_in = 1.0 / math.sqrt(depth)
    normed = normalize(rows)
    first = lax.axis_index("fsdp") * width
    column = lax.dynamic_slice_in_dim(rows, first, width, 1).astype(f32)
    following = jnp.concatenate([column[1:], jnp.zeros((1, width), f32)], 0)
    predicted = jnp.dot(normed, weight, preferred_element_type=f32) * scale_in + column
    inside = lax.iota(jnp.int32, rows.shape[0]) < rows.shape[0] - 1
    residual = jnp.where(inside[:, None], predicted - following, 0.0).astype(bf16)
    gradient = scale_in * lax.dot_general(
        normed, residual, (((0,), (0,)), ((), ())), preferred_element_type=f32
    )
    count = depth * width * lax.axis_size("fsdp")
    return gradient, lax.rsqrt(fsdp_sum(jnp.sum(gradient * gradient)) / count + 1e-06)


def both_steps(bits, weight, moment, states):
    bit0, bit1 = bits
    side = (lax.axis_index("rep") >> bit1) & 1
    half = weight.shape[0] // 2

    def part(value, which):
        return lax.dynamic_slice_in_dim(value, which * half, half, 0)

    mine, other = side, 1 - side
    rows0 = lax.all_gather(states[0, 0], "fsdp", axis=0, tiled=True)
    combined = 0.5 * weight.astype(f32) - step_size * pair_keep * moment
    partner_combined = swapped(combined.astype(bf16), bit0)
    partner_half = swapped(part(moment, other).astype(bf16), bit1)
    pair_half = part(moment, mine) + partner_half.astype(f32)
    all_half = pair_half + swapped(pair_half.astype(bf16), bit0).astype(f32)
    rows1 = lax.all_gather(states[1, 0], "fsdp", axis=0, tiled=True)

    gradient0, factor0 = gradient_of(rows0, weight)
    update0 = gradient0 * factor0
    weight1 = (combined + partner_combined.astype(f32) - step_size * update0).astype(bf16)
    change0 = (weight1.astype(f32) - weight.astype(f32)).astype(bf16)

    base = 0.5 * weight1.astype(f32) - step_size * pair_keep * update0
    base_other = part(base, other)
    base_mine = part(base, mine) - step_size * pair_keep * pair_keep * all_half
    got_mine = swapped(base_other.astype(bf16), bit1)
    got_other = swapped(base_mine.astype(bf16), bit1)

    gradient1, factor1 = gradient_of(rows1, weight1)
    change1 = jnp.zeros_like(change0)
    for which, own, got in ((mine, base_mine, got_mine), (other, base_other, got_other)):
        new = (own + got.astype(f32) - step_size * (part(gradient1, which) * factor1)).astype(bf16)
        change = (new.astype(f32) - part(weight1, which).astype(f32)).astype(bf16)
        change1 = lax.dynamic_update_slice_in_dim(change1, change, which * half, 0)
    return jnp.stack([change0, change1])[:, None]


def local(weights, momentum, states, plan):
    levels = lax.axis_size("rep").bit_length() - 1
    top = levels - 1
    cases = [(top, low) for low in range(top)] + [(low, top) for low in range(top)]
    top_last = (plan[1] >= (1 << top)).astype(jnp.int32)
    smaller = jnp.minimum(plan[0], plan[1])
    index = top_last * top
    for bit in range(1, top):
        index = index + (smaller >= 1 << bit).astype(jnp.int32)
    return lax.switch(
        index, [partial(both_steps, bits) for bits in cases], weights[0], momentum[0], states
    )


def solution(mesh):
    placed = (P("rep", None, "fsdp"), P("rep", None, "fsdp"), P(None, "rep", "fsdp", None), P())
    return jax.shard_map(
        local, mesh=mesh, in_specs=placed, out_specs=P(None, "rep", None, "fsdp"), check_vma=False
    )
```

```python
import math

import jax
import jax.numpy as jnp
from jax import lax
from jax.sharding import PartitionSpec as P

step_size = 0.1
moment_keep = 0.9
pair_keep = 0.5 * moment_keep
f32 = jnp.float32
bf16 = jnp.bfloat16


def swapped(value, bit):
    mask = 2**bit
    pairs = [(source, source ^ mask) for source in range(lax.axis_size("rep"))]
    return lax.ppermute(value, "rep", pairs)


def normalize(row_block):
    values = row_block.astype(f32)
    return (values * lax.rsqrt(jnp.mean(values * values, axis=-1, keepdims=True) + 1e-06)).astype(bf16)


def fsdp_sum(value):
    size = lax.axis_size("fsdp")
    tile = jnp.full((8, 128), value, f32)
    total = tile
    for shift in range(1, size):
        total = total + lax.ppermute(tile, "fsdp", [(s, (s + shift) % size) for s in range(size)])
    return total[0, 0]


def gradient_of(rows, weight):
    depth, width = weight.shape
    scale_in = 1.0 / math.sqrt(depth)
    normed = normalize(rows)
    first = lax.axis_index("fsdp") * width
    column = lax.dynamic_slice_in_dim(rows, first, width, 1).astype(f32)
    following = jnp.concatenate([column[1:], jnp.zeros((1, width), f32)], 0)
    predicted = jnp.dot(normed, weight, preferred_element_type=f32) * scale_in + column
    inside = lax.iota(jnp.int32, rows.shape[0]) < rows.shape[0] - 1
    residual = jnp.where(inside[:, None], predicted - following, 0.0).astype(bf16)
    gradient = scale_in * lax.dot_general(
        normed, residual, (((0,), (0,)), ((), ())), preferred_element_type=f32
    )
    count = depth * width * lax.axis_size("fsdp")
    return gradient, lax.rsqrt(fsdp_sum(jnp.sum(gradient * gradient)) / count + 1e-06)


def local(weights, momentum, states, plan):
    weight, moment = weights[0], momentum[0]
    top = lax.axis_size("rep").bit_length() - 2
    top_last = plan[1] > plan[0]
    smaller = jnp.minimum(plan[0], plan[1])
    half = weight.shape[0] // 2

    def exchanged(first, second):
        to_top = jnp.where(top_last, second, first).astype(bf16)
        to_low = jnp.where(top_last, first, second).astype(bf16)
        from_top = swapped(to_top, top)
        from_low = swapped(to_low, 0)
        for bit in range(1, top):
            from_low = jnp.where(smaller == 1 << bit, swapped(to_low, bit), from_low)
        return jnp.where(top_last, from_low, from_top), jnp.where(top_last, from_top, from_low)

    def part(value, which):
        return lax.dynamic_slice_in_dim(value, which * half, half, 0)

    mine = ((lax.axis_index("rep") & plan[1]) > 0).astype(jnp.int32)
    other = 1 - mine
    rows0 = lax.all_gather(states[0, 0], "fsdp", axis=0, tiled=True)
    rows1 = lax.all_gather(states[1, 0], "fsdp", axis=0, tiled=True)

    combined = 0.5 * weight.astype(f32) - step_size * pair_keep * moment
    got_low_rows, got_moment = exchanged(combined[:half], part(moment, other))
    got_high_rows, _ = exchanged(combined[half:], combined[half:])
    pair_half = part(moment, mine) + got_moment.astype(f32)

    gradient0, factor0 = gradient_of(rows0, weight)
    update0 = gradient0 * factor0
    partner_combined = jnp.concatenate([got_low_rows, got_high_rows], 0).astype(f32)
    weight1 = (combined + partner_combined - step_size * update0).astype(bf16)
    change0 = (weight1.astype(f32) - weight.astype(f32)).astype(bf16)

    base = 0.5 * weight1.astype(f32) - step_size * pair_keep * update0
    base_other = part(base, other)
    got_pair, got_mine = exchanged(pair_half, base_other)
    all_half = pair_half + got_pair.astype(f32)
    base_mine = part(base, mine) - step_size * pair_keep * pair_keep * all_half
    sent_mine = base_mine.astype(bf16)
    _, got_other = exchanged(sent_mine, sent_mine)

    rows1, _ = lax.optimization_barrier((rows1, sent_mine))
    gradient1, factor1 = gradient_of(rows1, weight1)
    changes = jnp.zeros((2, 1) + weight.shape, bf16)
    changes = lax.dynamic_update_slice(changes, change0[None, None], (0, 0, 0, 0))
    for which, own, got in ((mine, base_mine, got_mine), (other, base_other, got_other)):
        new = (own + got.astype(f32) - step_size * (part(gradient1, which) * factor1)).astype(bf16)
        change = (new.astype(f32) - part(weight1, which).astype(f32)).astype(bf16)
        changes = lax.dynamic_update_slice(changes, change[None, None], (1, 0, which * half, 0))
    return changes


def solution(mesh):
    placed = (P("rep", None, "fsdp"), P("rep", None, "fsdp"), P(None, "rep", "fsdp", None), P())
    return jax.shard_map(
        local, mesh=mesh, in_specs=placed, out_specs=P(None, "rep", None, "fsdp"), check_vma=False
    )
```

```python
import math

import jax
import jax.numpy as jnp
from jax import lax
from jax.sharding import PartitionSpec as P

step_size = 0.1
moment_keep = 0.9
pair_keep = 0.5 * moment_keep
f32 = jnp.float32
bf16 = jnp.bfloat16


def swapped(value, bit):
    mask = 2**bit
    pairs = [(source, source ^ mask) for source in range(lax.axis_size("rep"))]
    return lax.ppermute(value, "rep", pairs)


def normalize(row_block):
    values = row_block.astype(f32)
    return (values * lax.rsqrt(jnp.mean(values * values, axis=-1, keepdims=True) + 1e-06)).astype(bf16)


def fsdp_sum(value):
    size = lax.axis_size("fsdp")
    tile = jnp.full((8, 128), value, f32)
    total = tile
    for shift in range(1, size):
        total = total + lax.ppermute(tile, "fsdp", [(s, (s + shift) % size) for s in range(size)])
    return total[0, 0]


def gradient_of(rows, weight):
    depth, width = weight.shape
    scale_in = 1.0 / math.sqrt(depth)
    normed = normalize(rows)
    first = lax.axis_index("fsdp") * width
    column = lax.dynamic_slice_in_dim(rows, first, width, 1).astype(f32)
    following = jnp.concatenate([column[1:], jnp.zeros((1, width), f32)], 0)
    predicted = jnp.dot(normed, weight, preferred_element_type=f32) * scale_in + column
    inside = lax.iota(jnp.int32, rows.shape[0]) < rows.shape[0] - 1
    residual = jnp.where(inside[:, None], predicted - following, 0.0).astype(bf16)
    gradient = scale_in * lax.dot_general(
        normed, residual, (((0,), (0,)), ((), ())), preferred_element_type=f32
    )
    count = depth * width * lax.axis_size("fsdp")
    return gradient, lax.rsqrt(fsdp_sum(jnp.sum(gradient * gradient)) / count + 1e-06)


def local(weights, momentum, states, plan):
    weight, moment = weights[0], momentum[0]
    top = lax.axis_size("rep").bit_length() - 2
    top_last = plan[1] > plan[0]
    smaller = jnp.minimum(plan[0], plan[1])
    half = weight.shape[0] // 2

    def exchanged(first, second):
        to_top = jnp.where(top_last, second, first).astype(bf16)
        to_low = jnp.where(top_last, first, second).astype(bf16)
        from_top = swapped(to_top, top)
        from_low = swapped(to_low, 0)
        for bit in range(1, top):
            from_low = jnp.where(smaller == 1 << bit, swapped(to_low, bit), from_low)
        return (
            jnp.where(top_last, from_low, from_top),
            jnp.where(top_last, from_top, from_low),
            (to_top, to_low),
        )

    def part(value, which):
        return lax.dynamic_slice_in_dim(value, which * half, half, 0)

    def after(value, earlier):
        return lax.optimization_barrier((value, earlier))[0]

    def combined(weight, moment, which):
        return 0.5 * part(weight, which).astype(f32) - step_size * pair_keep * part(moment, which)

    mine = ((lax.axis_index("rep") & plan[1]) > 0).astype(jnp.int32)
    other = 1 - mine
    rows0 = lax.all_gather(states[0, 0], "fsdp", axis=0, tiled=True)
    rows1 = lax.all_gather(states[1, 0], "fsdp", axis=0, tiled=True)

    got_other, got_moment, sent1 = exchanged(
        combined(weight, moment, other), part(moment, other)
    )
    weight_b, moment_b = after((weight, moment), sent1)
    combined_mine = combined(weight_b, moment_b, mine)
    got_mine, _, sent2 = exchanged(combined_mine, combined_mine)
    weight_c, moment_c = after((weight, moment), sent2)

    gradient0, factor0 = gradient_of(rows0, weight)

    def step0(weight, moment, gradient, got, which):
        update = part(gradient, which) * factor0
        new = combined(weight, moment, which) + got.astype(f32) - step_size * update
        return new.astype(bf16), step_size * pair_keep * update

    weight1_other, pull_other = step0(weight_c, moment_c, gradient0, got_other, other)
    pair_half = part(moment_c, mine) + got_moment.astype(f32)
    got_pair, got1_mine, sent3 = exchanged(
        pair_half, 0.5 * weight1_other.astype(f32) - pull_other
    )
    got_mine, gradient0_d = after((got_mine, gradient0), sent3)
    weight1_mine, pull_mine = step0(weight_c, moment_c, gradient0_d, got_mine, mine)
    weight1 = jnp.zeros_like(weight)
    weight1 = lax.dynamic_update_slice_in_dim(weight1, weight1_other, other * half, 0)
    weight1 = lax.dynamic_update_slice_in_dim(weight1, weight1_mine, mine * half, 0)
    change0 = (weight1.astype(f32) - weight.astype(f32)).astype(bf16)

    gradient1, factor1 = gradient_of(after(rows1, sent3), weight1)
    got_pair, gradient1 = lax.optimization_barrier((got_pair, gradient1))
    all_half = pair_half + got_pair.astype(f32)
    base_other = 0.5 * weight1_other.astype(f32) - step_size * pair_keep * factor0 * part(gradient0, other)
    base_mine = (
        0.5 * weight1_mine.astype(f32)
        - step_size * pair_keep * factor0 * part(gradient0_d, mine)
        - step_size * pair_keep * pair_keep * all_half
    )
    _, got1_other, sent4 = exchanged(base_mine, base_mine)

    changes = jnp.zeros((2, 1) + weight.shape, bf16)
    changes = lax.dynamic_update_slice(changes, change0[None, None], (0, 0, 0, 0))
    for which, now, own, got in (
        (mine, weight1_mine, base_mine, got1_mine),
        (other, weight1_other, base_other, got1_other),
    ):
        new = (own + got.astype(f32) - step_size * (part(gradient1, which) * factor1)).astype(bf16)
        change = (new.astype(f32) - now.astype(f32)).astype(bf16)
        changes = lax.dynamic_update_slice(changes, change[None, None], (1, 0, which * half, 0))
    return changes


def solution(mesh):
    placed = (P("rep", None, "fsdp"), P("rep", None, "fsdp"), P(None, "rep", "fsdp", None), P())
    return jax.shard_map(
        local, mesh=mesh, in_specs=placed, out_specs=P(None, "rep", None, "fsdp"), check_vma=False
    )
```

```python
import math

import jax
import jax.numpy as jnp
from jax import lax
from jax.sharding import PartitionSpec as P

step_size = 0.1
moment_keep = 0.9
pair_keep = 0.5 * moment_keep
f32 = jnp.float32
bf16 = jnp.bfloat16


def swapped(value, bit):
    mask = 2**bit
    pairs = [(source, source ^ mask) for source in range(lax.axis_size("rep"))]
    return lax.ppermute(value, "rep", pairs)


def normalize(row_block):
    values = row_block.astype(f32)
    return (values * lax.rsqrt(jnp.mean(values * values, axis=-1, keepdims=True) + 1e-06)).astype(bf16)


def fsdp_sum(value):
    size = lax.axis_size("fsdp")
    tile = jnp.full((8, 128), value, f32)
    total = tile
    for shift in range(1, size):
        total = total + lax.ppermute(tile, "fsdp", [(s, (s + shift) % size) for s in range(size)])
    return total[0, 0]


def gradient_of(rows, weight):
    depth, width = weight.shape
    scale_in = 1.0 / math.sqrt(depth)
    normed = normalize(rows)
    first = lax.axis_index("fsdp") * width
    column = lax.dynamic_slice_in_dim(rows, first, width, 1).astype(f32)
    following = jnp.concatenate([column[1:], jnp.zeros((1, width), f32)], 0)
    predicted = jnp.dot(normed, weight, preferred_element_type=f32) * scale_in + column
    inside = lax.iota(jnp.int32, rows.shape[0]) < rows.shape[0] - 1
    residual = jnp.where(inside[:, None], predicted - following, 0.0).astype(bf16)
    gradient = scale_in * lax.dot_general(
        normed, residual, (((0,), (0,)), ((), ())), preferred_element_type=f32
    )
    count = depth * width * lax.axis_size("fsdp")
    return gradient, lax.rsqrt(fsdp_sum(jnp.sum(gradient * gradient)) / count + 1e-06)


def local(weights, momentum, states, plan):
    weight, moment = weights[0], momentum[0]
    top = lax.axis_size("rep").bit_length() - 2
    top_last = plan[1] > plan[0]
    smaller = jnp.minimum(plan[0], plan[1])
    half = weight.shape[0] // 2

    def exchanged(first, second):
        to_top = jnp.where(top_last, second, first).astype(bf16)
        to_low = jnp.where(top_last, first, second).astype(bf16)
        from_top = swapped(to_top, top)
        from_low = swapped(to_low, 0)
        for bit in range(1, top):
            from_low = jnp.where(smaller == 1 << bit, swapped(to_low, bit), from_low)
        return (
            jnp.where(top_last, from_low, from_top),
            jnp.where(top_last, from_top, from_low),
            (to_top, to_low),
        )

    def part(value, which):
        return lax.dynamic_slice_in_dim(value, which * half, half, 0)

    def after(value, earlier):
        return lax.optimization_barrier((value, earlier))[0]

    def combined(weight, moment, which):
        return 0.5 * part(weight, which).astype(f32) - step_size * pair_keep * part(moment, which)

    mine = ((lax.axis_index("rep") & plan[1]) > 0).astype(jnp.int32)
    other = 1 - mine
    rows0 = lax.all_gather(states[0, 0], "fsdp", axis=0, tiled=True)
    rows1 = lax.all_gather(states[1, 0], "fsdp", axis=0, tiled=True)

    mine_combined = combined(weight, moment, mine)
    got_first, got_second, sent1 = exchanged(
        jnp.stack([combined(weight, moment, other), mine_combined]),
        jnp.stack([part(moment, other), mine_combined]),
    )
    got_other, got_mine, got_moment = got_first[0], got_first[1], got_second[0]
    weight_c, moment_c, rows0 = after((weight, moment, rows0), sent1)

    gradient0, factor0 = gradient_of(rows0, weight)

    def step0(weight, moment, gradient, got, which):
        update = part(gradient, which) * factor0
        new = combined(weight, moment, which) + got.astype(f32) - step_size * update
        return new.astype(bf16), step_size * pair_keep * update

    weight1_other, pull_other = step0(weight_c, moment_c, gradient0, got_other, other)
    pair_half = part(moment_c, mine) + got_moment.astype(f32)
    got_pair, got1_mine, sent3 = exchanged(
        pair_half, 0.5 * weight1_other.astype(f32) - pull_other
    )
    gradient0_d = after(gradient0, sent3)
    weight1_mine, pull_mine = step0(weight_c, moment_c, gradient0_d, got_mine, mine)
    weight1 = jnp.zeros_like(weight)
    weight1 = lax.dynamic_update_slice_in_dim(weight1, weight1_other, other * half, 0)
    weight1 = lax.dynamic_update_slice_in_dim(weight1, weight1_mine, mine * half, 0)
    change0 = (weight1.astype(f32) - weight.astype(f32)).astype(bf16)

    got_pair, change0, rows1 = lax.optimization_barrier((got_pair, change0, rows1))
    all_half = pair_half + got_pair.astype(f32)
    base_other = 0.5 * weight1_other.astype(f32) - step_size * pair_keep * factor0 * part(gradient0, other)
    base_mine = (
        0.5 * weight1_mine.astype(f32)
        - step_size * pair_keep * factor0 * part(gradient0_d, mine)
        - step_size * pair_keep * pair_keep * all_half
    )
    _, got1_other, sent4 = exchanged(base_mine, base_mine)

    gradient1, factor1 = gradient_of(rows1, after(weight1, sent4))
    changes = jnp.zeros((2, 1) + weight.shape, bf16)
    changes = lax.dynamic_update_slice(changes, change0[None, None], (0, 0, 0, 0))
    for which, now, own, got in (
        (mine, weight1_mine, base_mine, got1_mine),
        (other, weight1_other, base_other, got1_other),
    ):
        new = (own + got.astype(f32) - step_size * (part(gradient1, which) * factor1)).astype(bf16)
        change = (new.astype(f32) - now.astype(f32)).astype(bf16)
        changes = lax.dynamic_update_slice(changes, change[None, None], (1, 0, which * half, 0))
    return changes


def solution(mesh):
    placed = (P("rep", None, "fsdp"), P("rep", None, "fsdp"), P(None, "rep", "fsdp", None), P())
    return jax.shard_map(
        local, mesh=mesh, in_specs=placed, out_specs=P(None, "rep", None, "fsdp"), check_vma=False
    )
```

```python
import math

import jax
import jax.numpy as jnp
from jax import lax
from jax.sharding import PartitionSpec as P

step_size = 0.1
moment_keep = 0.9
pair_keep = 0.5 * moment_keep
f32 = jnp.float32
bf16 = jnp.bfloat16


def swapped(value, bit):
    mask = 2**bit
    pairs = [(source, source ^ mask) for source in range(lax.axis_size("rep"))]
    return lax.ppermute(value, "rep", pairs)


def normalize(row_block):
    values = row_block.astype(f32)
    return (values * lax.rsqrt(jnp.mean(values * values, axis=-1, keepdims=True) + 1e-06)).astype(bf16)


def fsdp_sum(value):
    size = lax.axis_size("fsdp")
    tile = jnp.full((8, 128), value, f32)
    total = tile
    for shift in range(1, size):
        total = total + lax.ppermute(tile, "fsdp", [(s, (s + shift) % size) for s in range(size)])
    return total[0, 0]


def gradient_of(rows, weight):
    depth, width = weight.shape
    scale_in = 1.0 / math.sqrt(depth)
    normed = normalize(rows)
    first = lax.axis_index("fsdp") * width
    column = lax.dynamic_slice_in_dim(rows, first, width, 1).astype(f32)
    following = jnp.concatenate([column[1:], jnp.zeros((1, width), f32)], 0)
    predicted = jnp.dot(normed, weight, preferred_element_type=f32) * scale_in + column
    inside = lax.iota(jnp.int32, rows.shape[0]) < rows.shape[0] - 1
    residual = jnp.where(inside[:, None], predicted - following, 0.0).astype(bf16)
    gradient = scale_in * lax.dot_general(
        normed, residual, (((0,), (0,)), ((), ())), preferred_element_type=f32
    )
    count = depth * width * lax.axis_size("fsdp")
    return gradient, lax.rsqrt(fsdp_sum(jnp.sum(gradient * gradient)) / count + 1e-06)


def local(weights, momentum, states, plan):
    weight, moment = weights[0], momentum[0]
    top = lax.axis_size("rep").bit_length() - 2
    top_last = plan[1] > plan[0]
    smaller = jnp.minimum(plan[0], plan[1])
    half = weight.shape[0] // 2

    def exchanged(first, second):
        to_top = jnp.where(top_last, second, first).astype(bf16)
        to_low = jnp.where(top_last, first, second).astype(bf16)
        from_top = swapped(to_top, top)
        from_lows = [swapped(to_low, bit) for bit in range(top)]

        def answers(cut):
            low = cut(from_lows[0])
            for bit in range(1, top):
                low = jnp.where(smaller == 1 << bit, cut(from_lows[bit]), low)
            high = cut(from_top)
            return jnp.where(top_last, low, high), jnp.where(top_last, high, low)

        if first.ndim == 2:
            return *answers(lambda array: array), (to_top, to_low)
        return answers(lambda array: array[0]), answers(lambda array: array[1]), (to_top, to_low)

    def part(value, which):
        return lax.dynamic_slice_in_dim(value, which * half, half, 0)

    def after(value, earlier):
        return lax.optimization_barrier((value, earlier))[0]

    def combined(weight, moment, which):
        return 0.5 * part(weight, which).astype(f32) - step_size * pair_keep * part(moment, which)

    mine = ((lax.axis_index("rep") & plan[1]) > 0).astype(jnp.int32)
    other = 1 - mine
    rows0 = lax.all_gather(states[0, 0], "fsdp", axis=0, tiled=True)
    rows1 = lax.all_gather(states[1, 0], "fsdp", axis=0, tiled=True)

    mine_combined = combined(weight, moment, mine)
    got_halves0, got_halves1, sent1 = exchanged(
        jnp.stack([combined(weight, moment, other), mine_combined]),
        jnp.stack([part(moment, other), mine_combined]),
    )
    (got_other, got_moment), (got_mine, _) = got_halves0, got_halves1
    weight_c, moment_c, rows0 = after((weight, moment, rows0), sent1)

    gradient0, factor0 = gradient_of(rows0, weight)

    def step0(weight, moment, gradient, got, which):
        update = part(gradient, which) * factor0
        new = combined(weight, moment, which) + got.astype(f32) - step_size * update
        return new.astype(bf16), step_size * pair_keep * update

    weight1_other, pull_other = step0(weight_c, moment_c, gradient0, got_other, other)
    pair_half = part(moment_c, mine) + got_moment.astype(f32)
    got_pair, got1_mine, sent3 = exchanged(
        pair_half, 0.5 * weight1_other.astype(f32) - pull_other
    )
    gradient0_d = after(gradient0, sent3)
    weight1_mine, pull_mine = step0(weight_c, moment_c, gradient0_d, got_mine, mine)
    weight1 = jnp.zeros_like(weight)
    weight1 = lax.dynamic_update_slice_in_dim(weight1, weight1_other, other * half, 0)
    weight1 = lax.dynamic_update_slice_in_dim(weight1, weight1_mine, mine * half, 0)
    change0 = (weight1.astype(f32) - weight.astype(f32)).astype(bf16)

    got_pair, change0, rows1 = lax.optimization_barrier((got_pair, change0, rows1))
    all_half = pair_half + got_pair.astype(f32)
    base_other = 0.5 * weight1_other.astype(f32) - step_size * pair_keep * factor0 * part(gradient0, other)
    base_mine = (
        0.5 * weight1_mine.astype(f32)
        - step_size * pair_keep * factor0 * part(gradient0_d, mine)
        - step_size * pair_keep * pair_keep * all_half
    )
    _, got1_other, sent4 = exchanged(base_mine, base_mine)

    gradient1, factor1 = gradient_of(rows1, after(weight1, sent4))
    changes = jnp.zeros((2, 1) + weight.shape, bf16)
    changes = lax.dynamic_update_slice(changes, change0[None, None], (0, 0, 0, 0))
    for which, now, own, got in (
        (mine, weight1_mine, base_mine, got1_mine),
        (other, weight1_other, base_other, got1_other),
    ):
        new = (own + got.astype(f32) - step_size * (part(gradient1, which) * factor1)).astype(bf16)
        change = (new.astype(f32) - now.astype(f32)).astype(bf16)
        changes = lax.dynamic_update_slice(changes, change[None, None], (1, 0, which * half, 0))
    return changes


def solution(mesh):
    placed = (P("rep", None, "fsdp"), P("rep", None, "fsdp"), P(None, "rep", "fsdp", None), P())
    return jax.shard_map(
        local, mesh=mesh, in_specs=placed, out_specs=P(None, "rep", None, "fsdp"), check_vma=False
    )
```
